32 devices in a mesh: space: 4 (over y, x), mom: 8 (over z, core).
Axes of the slice: x: 2, y: 2, z: 4, core: 2. Of those that a mesh axis runs over, the one named last changes fastest.
Arguments:
- density: float32 [256, 256, 512], P('mom', None, 'space'), may hold values from -6 to 6
- mode_waves: int32 [16, 2], replicated, may hold values from -7 to 7
- mode_amplitudes: float32 [16], replicated, may hold values from -3 to 3
- mode_phases: float32 [16], replicated, may hold values from -3.140625 to 3.140625
Outputs:
- time_rate: float32 [256, 256, 512], P('mom', None, 'space')
The draws below stay inside these ranges and needn't reach their ends.
All inputs are finite; a program needn't handle non-finite values.
Results may differ from the reference program's by a relative error of at most 0.0003.
Values sent between devices are 32-bit elements; how exact they have to be, the bound alone decides.
A program may use at most 128 MiB of HBM per device.

```python
import math
import jax
import jax.numpy as jnp
from jax import lax

P_SIZE = 256
NY = 16
RX = 8
MODES = 16
NX = 32
CELLS = 512
N_SPACE = 4


def set_ends(result, rng, least, top_value):
    dims = result.shape
    spot = [jax.random.randint(jax.random.fold_in(rng, axis), (), 0, dims[axis]) for axis in range(len(dims))]
    result = result.at[tuple(spot)].set(least)
    longest = dims.index(max(dims))
    spot[longest] = (spot[longest] + 1) % dims[longest]
    return result.at[tuple(spot)].set(top_value)


def shard_levels(rng, dims, shards, least, top_value):
    loudness = 1.0
    for axis_at, blocks in shards:
        draws = jax.random.uniform(jax.random.fold_in(jax.random.fold_in(rng, 6), axis_at), (blocks,), jnp.float32, least / len(shards), top_value / len(shards))
        loudness = loudness * jnp.repeat(jnp.exp(draws), dims[axis_at] // blocks).reshape((-1,) + (1,) * (len(dims) - 1 - axis_at))
    return loudness


def bell_draw(stream_key, dims, scale, bound, shards=(), kind=jnp.bfloat16):
    loudness = shard_levels(stream_key, dims, shards, -0.22, 0.18) if shards else 1.0
    drawn = jax.random.normal(stream_key, dims, jnp.float32) * scale * loudness
    return jnp.minimum(jnp.maximum(drawn, -bound), bound).astype(kind)


def setup_inputs(seed: int = 0) -> dict:
    key_of = jax.random.split(jax.random.key(seed), 5)
    density = bell_draw(key_of[0], (P_SIZE, P_SIZE, CELLS), 1.0, 6.0, ((0, 8), (2, 4)), jnp.float32)
    mode_waves = set_ends(jax.random.randint(key_of[1], (MODES, 2), -7, 8), jax.random.fold_in(key_of[1], 1), -7, 7).astype(jnp.int32)
    mode_amplitudes = bell_draw(key_of[2], (MODES,), 0.5, 3.0, (), jnp.float32)
    mode_phases = jnp.clip(jax.random.uniform(key_of[3], (MODES,), jnp.float32, -3.140625, 3.140625), -3.140625, 3.140625)
    return {"density": density, "mode_waves": mode_waves, "mode_amplitudes": mode_amplitudes, "mode_phases": mode_phases}


HIGHEST_PRECISION = lax.Precision.HIGHEST
DAMPING = 0.5
FRICTION = 0.5


def velocity(indices, points):
    return (2 * indices - points + 1).astype(jnp.float32) / points


def signed_frequency(indices, points):
    return jnp.where(indices < points // 2, indices, indices - points)


def cell_factors(mode_waves, mode_amplitudes, mode_phases, row_number, column_number, total_rows, total_columns):
    turn_rows = (mode_waves[:, 0:1] * row_number[None, :]) % total_rows
    turn_columns = (mode_waves[:, 1:2] * column_number[None, :]) % total_columns
    angles = 2.0 * math.pi * (turn_rows.astype(jnp.float32) / total_rows + turn_columns.astype(jnp.float32) / total_columns) + mode_phases[:, None]
    return mode_amplitudes[:, None] * jnp.sin(angles)


def freq_factors(mode_waves, first_freq, second_freq, points):
    summed = (mode_waves[None, None, :, 0] * first_freq[:, None, None] + mode_waves[None, None, :, 1] * second_freq[None, :, None]) % (2 * points)
    values = jnp.sin((math.pi / points) * summed.astype(jnp.float32))
    return values.reshape(first_freq.shape[0] * second_freq.shape[0], mode_waves.shape[0])


def damping_table(first_freq, second_freq, points):
    squares = first_freq[:, None] * first_freq[:, None] + second_freq[None, :] * second_freq[None, :]
    return (DAMPING / ((points // 2) * (points // 2))) * squares.astype(jnp.float32)


def upwind(shifted):
    minus_side = (-2.0 * shifted(-3) + 15.0 * shifted(-2) - 60.0 * shifted(-1) + 20.0 * shifted(0) + 30.0 * shifted(1) - 3.0 * shifted(2)) / 60.0
    plus_side = (2.0 * shifted(3) - 15.0 * shifted(2) + 60.0 * shifted(1) - 20.0 * shifted(0) - 30.0 * shifted(-1) + 3.0 * shifted(-2)) / 60.0
    return minus_side, plus_side


def friction_term(values, row_speeds, column_speeds):
    weighted_rows = row_speeds[:, None, None] * values
    weighted_columns = column_speeds[None, :, None] * values
    padded_rows = jnp.pad(weighted_rows, ((1, 1), (0, 0), (0, 0)))
    padded_columns = jnp.pad(weighted_columns, ((0, 0), (1, 1), (0, 0)))
    return FRICTION * ((padded_rows[2:] - padded_rows[:-2]) + (padded_columns[:, 2:] - padded_columns[:, :-2]))


def reference(density, mode_waves, mode_amplitudes, mode_phases):
    points = P_SIZE
    band_cells = RX * NY
    indices = jnp.arange(points, dtype=jnp.int32)
    signed = signed_frequency(indices, points)
    freq_factor = freq_factors(mode_waves, signed, signed, points)
    damping = damping_table(signed, signed, points)
    speeds = velocity(indices, points)

    def band_part(band_index):
        offset = (band_index * band_cells).astype(jnp.int32)
        sliced = lax.dynamic_slice_in_dim(density, offset, band_cells, 2)
        cell_ids = offset + jnp.arange(band_cells, dtype=jnp.int32)
        cell_factor = cell_factors(mode_waves, mode_amplitudes, mode_phases, cell_ids // NY, cell_ids % NY, NX, NY)
        symbol = jnp.dot(freq_factor, cell_factor, precision=HIGHEST_PRECISION).reshape(points, points, band_cells)
        spectrum = jnp.fft.fft2(sliced, axes=(0, 1))
        spectral = jnp.real(jnp.fft.ifft2((1j * symbol - damping[:, :, None]) * spectrum, axes=(0, 1)))
        return spectral + friction_term(sliced, speeds, speeds)

    momentum_part = lax.map(band_part, jnp.arange(N_SPACE, dtype=jnp.int32))

    def plane_rate(plane):
        values = lax.dynamic_index_in_dim(density, plane, 0, keepdims=False)
        moment_plane = lax.dynamic_index_in_dim(momentum_part, plane, 1, keepdims=False)
        moment_plane = jnp.moveaxis(moment_plane, 0, 1).reshape(points, CELLS)

        def across(offset):
            return jnp.roll(values, -offset * NY, axis=1)

        cell_grid = values.reshape(points, NX, NY)

        def along_row(offset):
            return jnp.roll(cell_grid, -offset, axis=2).reshape(points, CELLS)

        minus_rows, plus_rows = upwind(across)
        minus_columns, plus_columns = upwind(along_row)
        speed_rows = lax.dynamic_index_in_dim(speeds, plane, 0, keepdims=True)[:, None]
        speed_columns = speeds[:, None]
        advection = speed_rows * jnp.where(speed_rows > 0, minus_rows, plus_rows) + speed_columns * jnp.where(speed_columns > 0, minus_columns, plus_columns)
        return moment_plane - advection

    return lax.map(plane_rate, indices)
```

```python
import functools

import jax
import jax.numpy as jnp
import ml_dtypes
import numpy as np
from jax import lax
from jax.experimental import pallas as pl
from jax.experimental.pallas import tpu as pltpu
from jax.sharding import PartitionSpec as P

NY = 16
PER = 4
ROWS = 2 * PER
DAMPING = 0.5
FRICTION = 0.5
BF16 = jnp.bfloat16
F32 = jnp.float32
MINUS = ((-3, -2.0), (-2, 15.0), (-1, -60.0), (0, 20.0), (1, 30.0), (2, -3.0))
PLUS = ((3, 2.0), (2, -15.0), (1, 60.0), (0, -20.0), (-1, -30.0), (-2, 3.0))


def halves(table):
    high = table.astype(ml_dtypes.bfloat16)
    low = (table - high.astype(np.float64)).astype(ml_dtypes.bfloat16)
    return jnp.asarray(high), jnp.asarray(low)


def mode_order(points, peers):
    per_peer = points // 2 // peers
    return [
        d * per_peer + c * PER + i
        for c in range(per_peer // PER)
        for d in range(peers)
        for i in range(PER)
    ]


def second_tables(points, peers):
    k = np.arange(points)
    forward, back = [], []
    for m in mode_order(points, peers):
        angle = 2.0 * np.pi / points * (k * m % points)
        if m == 0:
            sign = 1.0 - 2.0 * (k % 2)
            forward += [np.ones(points), sign]
            back += [np.ones(points) / points, sign / points]
        else:
            forward += [np.cos(angle), -np.sin(angle)]
            back += [2.0 / points * np.cos(angle), -2.0 / points * np.sin(angle)]
    return np.stack(forward), np.stack(back).T.copy()


def first_tables(points):
    k = np.arange(points)
    turned = k[:, None] * k[None, :] % points
    cosine = np.cos(2.0 * np.pi / points * turned)
    sine = np.sin(2.0 * np.pi / points * turned)
    sine[turned * 2 % points == 0] = 0.0
    return np.concatenate([cosine, sine], 0), np.concatenate([cosine, sine], 1) / points


def row_tables(cells, stencil):
    own = np.zeros((cells, cells))
    left = np.zeros((2, cells, cells))
    right = np.zeros((2, cells, cells))
    half = cells // 2
    for n in range(cells):
        for s, w in stencil:
            src = n + s * NY
            if src < 0:
                for h in range(2):
                    left[h, src + half + h * half, n] += w
            elif src >= cells:
                for h in range(2):
                    right[h, src - cells + h * half, n] += w
            else:
                own[src, n] += w
    return own, np.concatenate(list(left), 1), np.concatenate(list(right), 1)


def column_table(cells, stencil):
    table = np.zeros((cells, cells))
    for n in range(cells):
        for s, w in stencil:
            table[n // NY * NY + (n % NY + s) % NY, n] += w
    return table


def split(value):
    high = value.astype(BF16)
    return high, (value - high.astype(F32)).astype(BF16)


def mm(a, b):
    return jnp.dot(a, b, preferred_element_type=F32)


def left_product(high, low, value):
    vh, vl = split(value)
    return mm(high, vh) + (mm(high, vl) + mm(low, vh))


def exact_product(value, table):
    vh, vl = split(value)
    return mm(vh, table) + mm(vl, table)


def forward_kernel(count, peers, block, x_ref, wh_ref, wl_ref, *outs):
    for a in range(block):
        y = left_product(wh_ref[...], wl_ref[...], x_ref[a])
        for c in range(count):
            for d in range(peers):
                at = (c * peers + d) * ROWS
                outs[c][d, a] = y[at : at + ROWS]


def middle_kernel(
    special, points, cells, flag_ref, x_ref, th_ref, tl_ref, ih_ref, il_ref, a_ref, b_ref, dm_ref, y_ref
):
    row = lax.broadcasted_iota(jnp.int32, (points, 2 * cells), 0)
    speed = (2 * row - (points - 1)).astype(F32) * (FRICTION / points)
    for i in range(PER):
        re = x_ref[pl.ds(2 * i, points, stride=ROWS), :]
        im = x_ref[pl.ds(2 * i + 1, points, stride=ROWS), :]
        x = jnp.concatenate([re, im], axis=1)
        pq = left_product(th_ref[...], tl_ref[...], x)
        pr, pi = pq[:points, :cells], pq[:points, cells:]
        qr, qi = pq[points:, :cells], pq[points:, cells:]
        s = jnp.dot(a_ref[...], b_ref[i], precision=lax.Precision.HIGHEST, preferred_element_type=F32)
        d = dm_ref[i]
        xr, xi = pr + qi, pi - qr
        ur = -d * xr - s * xi
        ui = s * xr - d * xi
        vr, vi = -ui, ur
        if special and i == 0:
            last = jnp.dot(
                a_ref[...], b_ref[PER], precision=lax.Precision.HIGHEST, preferred_element_type=F32
            )
            dl = dm_ref[PER]
            chosen = flag_ref[0] == 0
            ur = jnp.where(chosen, s * qr - d * pr, ur)
            ui = jnp.where(chosen, last * qi - dl * pi, ui)
            vr = jnp.where(chosen, -d * qr - s * pr, vr)
            vi = jnp.where(chosen, -dl * qi - last * pi, vi)
        u = jnp.concatenate([ur, ui], axis=1)
        v = jnp.concatenate([vr, vi], axis=1)
        y = left_product(ih_ref[...], il_ref[...], jnp.concatenate([u, v], axis=0))
        weighted = speed * x
        above = jnp.where(row < points - 1, pltpu.roll(weighted, points - 1, 0), 0.0)
        below = jnp.where(row > 0, pltpu.roll(weighted, 1, 0), 0.0)
        y = y + (above - below)
        y_ref[pl.ds(2 * i, points, stride=ROWS), :] = y[:, :cells]
        y_ref[pl.ds(2 * i + 1, points, stride=ROWS), :] = y[:, cells:]


def local_kernel(points, cells, block, x_ref, l_ref, r_ref, sp_ref, plus_ref, minus_ref, lt_ref, rt_ref, o_ref):
    half = points // 2
    row = lax.broadcasted_iota(jnp.int32, (points, cells), 0)
    speed = (2 * row - (points - 1)).astype(F32) / points
    for a in range(block):
        x = x_ref[a]
        top = exact_product(x[:half], plus_ref[...])
        bottom = exact_product(x[half:], minus_ref[...])
        sides = exact_product(l_ref[a], lt_ref[...]) + exact_product(r_ref[a], rt_ref[...])
        rows = jnp.concatenate([top[:, :cells] + sides[:, :cells], bottom[:, :cells] + sides[:, cells:]], 0)
        columns = jnp.concatenate([top[:, cells:], bottom[:, cells:]], 0)
        weighted = speed * x
        above = jnp.where(row < points - 1, pltpu.roll(weighted, points - 1, 0), 0.0)
        below = jnp.where(row > 0, pltpu.roll(weighted, 1, 0), 0.0)
        first = sp_ref[a]
        o_ref[a] = FRICTION * (above - below) - (first * rows + speed * columns) * (1.0 / 60.0)


def back_kernel(chunks, peers, block, base_ref, wh_ref, wl_ref, *refs):
    ys, o_ref = refs[:chunks], refs[chunks]
    for a in range(block):
        y = jnp.concatenate([ys[c][d, a] for c in range(chunks) for d in range(peers)], axis=0)
        o_ref[a] = base_ref[a] + left_product(wh_ref[...], wl_ref[...], y)


def whole(shape):
    return pl.BlockSpec(shape, lambda *_: (0,) * len(shape))


def params(mib=48):
    return pltpu.CompilerParams(vmem_limit_bytes=mib * 2**20)


def cost(flops, size):
    return pl.CostEstimate(flops=int(flops), bytes_accessed=int(size), transcendentals=0)


def local(density, mode_waves, mode_amplitudes, mode_phases):
    plane_rows, points, cells = density.shape
    rows_dev = cells // NY
    peers = lax.axis_size("mom")
    bands = lax.axis_size("space")
    total_rows = rows_dev * bands
    mom = lax.axis_index("mom")
    space = lax.axis_index("space")
    per_peer = points // 2 // peers
    chunks = per_peer // PER
    block = 8
    steps = plane_rows // block
    half = points // 2
    size = plane_rows * points * cells * 4

    forward, back = second_tables(points, peers)
    bh, bl = halves(back)
    first, inverse = first_tables(points)
    th, tl = halves(first)
    ih, il = halves(inverse)

    def ahead(low, high):
        count = high - low
        part = points // chunks
        wh, wl = halves(forward[low * part : high * part])
        return pl.pallas_call(
            functools.partial(forward_kernel, count, peers, block),
            grid=(steps,),
            out_shape=[jax.ShapeDtypeStruct((peers, plane_rows, ROWS, cells), F32)] * count,
            in_specs=[
                pl.BlockSpec((block, points, cells), lambda g: (g, 0, 0)),
                whole(wh.shape),
                whole(wl.shape),
            ],
            out_specs=[pl.BlockSpec((peers, block, ROWS, cells), lambda g: (0, g, 0, 0))] * count,
            compiler_params=params(),
            cost_estimate=cost(6 * plane_rows * points * cells * part * count, 2 * size),
            name=f"second_transform_{low}",
        )(density, wh, wl)

    sent = list(ahead(0, 1))
    if chunks > 1:
        sent += list(ahead(1, chunks))

    index = jnp.arange(points, dtype=jnp.int32)
    signed = jnp.where(index < half, index, index - points)
    unit = np.float32(np.pi / points)
    a_angle = unit * (mode_waves[None, :, 0] * signed[:, None] % (2 * points)).astype(F32)
    a_sine = jnp.where(index[:, None] == half, 0.0, jnp.sin(a_angle))
    a_table = jnp.concatenate([a_sine, jnp.cos(a_angle)], axis=1)
    cell = jnp.arange(cells, dtype=jnp.int32)
    turn_rows = mode_waves[:, 0:1] * (space * rows_dev + cell // NY)[None, :] % total_rows
    turn_columns = mode_waves[:, 1:2] * (cell % NY)[None, :] % NY
    angles = (
        2.0 * np.pi * (turn_rows.astype(F32) / total_rows + turn_columns.astype(F32) / NY)
        + mode_phases[:, None]
    )
    cell_factor = mode_amplitudes[:, None] * jnp.sin(angles)

    def mode_factors(modes):
        b_angle = unit * (mode_waves[None, :, 1] * modes[:, None] % (2 * points)).astype(F32)
        waves = jnp.concatenate([jnp.cos(b_angle), jnp.sin(b_angle)], axis=1)
        return waves[:, :, None] * jnp.concatenate([cell_factor, cell_factor], axis=0)[None]

    def damping_of(modes):
        squares = (signed * signed)[None, :] + (modes * modes)[:, None]
        values = DAMPING / (half * half) * squares.astype(F32)
        return jnp.broadcast_to(values[:, :, None], (modes.shape[0], points, cells))

    flag = mom.astype(jnp.int32).reshape(1)

    def middle(c, value):
        modes = mom * per_peer + c * PER + jnp.arange(PER, dtype=jnp.int32)
        modes = jnp.concatenate([modes, jnp.full((1,), -half, jnp.int32)])
        vm = pl.BlockSpec(memory_space=pltpu.VMEM)
        return pl.pallas_call(
            functools.partial(middle_kernel, c == 0, points, cells),
            out_shape=jax.ShapeDtypeStruct((points * ROWS, cells), F32),
            in_specs=[pl.BlockSpec(memory_space=pltpu.SMEM)] + [vm] * 8,
            out_specs=vm,
            compiler_params=params(),
            cost_estimate=cost(3 * PER * 16 * points * points * cells, points * ROWS * cells * 12),
            name=f"first_transform_{c}",
        )(
            flag,
            value.reshape(points * ROWS, cells),
            th,
            tl,
            ih,
            il,
            a_table,
            mode_factors(modes),
            damping_of(modes),
        )

    def exchange(value):
        return lax.all_to_all(value, "mom", split_axis=0, concat_axis=0, tiled=True)

    arrived = [exchange(v) for v in sent]

    up = [(i, (i + 1) % bands) for i in range(bands)]
    down = [(j, i) for i, j in up]
    middle_cell = cells // 2

    def packed(part):
        return jnp.concatenate([part[:, :half], part[:, half:]], axis=2)

    before = lax.ppermute(packed(density[:, :, middle_cell:]), "space", up)
    after = lax.ppermute(packed(density[:, :, :middle_cell]), "space", down)
    positive = mom * plane_rows >= half
    own_m, left_m, right_m = row_tables(cells, MINUS)
    own_p, left_p, right_p = row_tables(cells, PLUS)

    def chosen(minus, plus):
        return jnp.where(positive, jnp.asarray(minus, BF16), jnp.asarray(plus, BF16))

    def beside(columns):
        return chosen(np.concatenate([own_m, columns], 1), np.concatenate([own_p, columns], 1))

    speeds = (2 * (mom * plane_rows + jnp.arange(plane_rows, dtype=jnp.int32)) - points + 1).astype(F32) / points
    speeds = jnp.broadcast_to(speeds[:, None, None], (plane_rows, 1, cells))
    plane = lambda g: (g, 0, 0)
    table = whole((cells, 2 * cells))
    base = pl.pallas_call(
        functools.partial(local_kernel, points, cells, block),
        grid=(steps,),
        out_shape=jax.ShapeDtypeStruct(density.shape, F32),
        in_specs=[
            pl.BlockSpec((block, points, cells), plane),
            pl.BlockSpec((block, half, cells), plane),
            pl.BlockSpec((block, half, cells), plane),
            pl.BlockSpec((block, 1, cells), plane),
            table,
            table,
            table,
            table,
        ],
        out_specs=pl.BlockSpec((block, points, cells), plane),
        compiler_params=params(),
        cost_estimate=cost(plane_rows * 16 * half * cells * 2 * cells, 3 * size),
        name="advection_friction",
    )(
        density,
        before,
        after,
        speeds,
        beside(column_table(cells, PLUS)),
        beside(column_table(cells, MINUS)),
        chosen(left_m, left_p),
        chosen(right_m, right_p),
    )

    returned = [
        exchange(middle(c, arrived[c]).reshape(peers, plane_rows, ROWS, cells)) for c in range(chunks)
    ]
    return pl.pallas_call(
        functools.partial(back_kernel, chunks, peers, block),
        grid=(steps,),
        out_shape=jax.ShapeDtypeStruct(density.shape, F32),
        in_specs=[
            pl.BlockSpec((block, points, cells), plane),
            whole(bh.shape),
            whole(bl.shape),
        ]
        + [pl.BlockSpec((peers, block, ROWS, cells), lambda g: (0, g, 0, 0))] * chunks,
        out_specs=pl.BlockSpec((block, points, cells), plane),
        compiler_params=params(),
        cost_estimate=cost(6 * plane_rows * points * points * cells, 3 * size),
        name="second_inverse",
    )(base, bh, bl, *returned)


def solution(mesh):
    return jax.shard_map(
        local,
        mesh=mesh,
        in_specs=(P("mom", None, "space"), P(), P(), P()),
        out_specs=P("mom", None, "space"),
        check_vma=False,
    )
```

```python
import functools

import jax
import jax.numpy as jnp
import ml_dtypes
import numpy as np
from jax import lax
from jax.experimental import pallas as pl
from jax.experimental.pallas import tpu as pltpu
from jax.sharding import PartitionSpec as P

NY = 16
PER = 4
ROWS = 2 * PER
DAMPING = 0.5
FRICTION = 0.5
BF16 = jnp.bfloat16
F32 = jnp.float32
MINUS = ((-3, -2.0), (-2, 15.0), (-1, -60.0), (0, 20.0), (1, 30.0), (2, -3.0))
PLUS = ((3, 2.0), (2, -15.0), (1, 60.0), (0, -20.0), (-1, -30.0), (-2, 3.0))


def halves(table):
    high = table.astype(ml_dtypes.bfloat16)
    low = (table - high.astype(np.float64)).astype(ml_dtypes.bfloat16)
    return jnp.asarray(high), jnp.asarray(low)


def mode_order(points, peers):
    per_peer = points // 2 // peers
    return [
        d * per_peer + c * PER + i
        for c in range(per_peer // PER)
        for d in range(peers)
        for i in range(PER)
    ]


def second_tables(points, peers):
    k = np.arange(points)
    forward, back = [], []
    for m in mode_order(points, peers):
        angle = 2.0 * np.pi / points * (k * m % points)
        if m == 0:
            sign = 1.0 - 2.0 * (k % 2)
            forward += [np.ones(points), sign]
            back += [np.ones(points) / points, sign / points]
        else:
            forward += [np.cos(angle), -np.sin(angle)]
            back += [2.0 / points * np.cos(angle), -2.0 / points * np.sin(angle)]
    return np.stack(forward), np.stack(back).T.copy()


def first_tables(points):
    k = np.arange(points)
    turned = k[:, None] * k[None, :] % points
    cosine = np.cos(2.0 * np.pi / points * turned)
    sine = np.sin(2.0 * np.pi / points * turned)
    sine[turned * 2 % points == 0] = 0.0
    return np.concatenate([cosine, sine], 0), np.concatenate([cosine, sine], 1) / points


def row_tables(cells, stencil):
    own = np.zeros((cells, cells))
    left = np.zeros((2, cells, cells))
    right = np.zeros((2, cells, cells))
    half = cells // 2
    for n in range(cells):
        for s, w in stencil:
            src = n + s * NY
            if src < 0:
                for h in range(2):
                    left[h, src + half + h * half, n] += w
            elif src >= cells:
                for h in range(2):
                    right[h, src - cells + h * half, n] += w
            else:
                own[src, n] += w
    return own, np.concatenate(list(left), 1), np.concatenate(list(right), 1)


def column_table(cells, stencil):
    table = np.zeros((cells, cells))
    for n in range(cells):
        for s, w in stencil:
            table[n // NY * NY + (n % NY + s) % NY, n] += w
    return table


def split(value):
    high = value.astype(BF16)
    return high, (value - high.astype(F32)).astype(BF16)


def mm(a, b):
    return jnp.dot(a, b, preferred_element_type=F32)


def left_product(high, low, value):
    vh, vl = split(value)
    return mm(high, vh) + (mm(high, vl) + mm(low, vh))


def exact_product(value, table):
    vh, vl = split(value)
    return mm(vh, table) + mm(vl, table)


def difference(weighted, row, points):
    above = jnp.where(row < points - 1, pltpu.roll(weighted, points - 1, 0), 0.0)
    below = jnp.where(row > 0, pltpu.roll(weighted, 1, 0), 0.0)
    return above - below


def exchange_kernel(
    peers,
    bands,
    chunks,
    plane_rows,
    points,
    cells,
    x_ref,
    wh_ref,
    wl_ref,
    th_ref,
    tl_ref,
    ih_ref,
    il_ref,
    a_ref,
    b_ref,
    plus_ref,
    minus_ref,
    lt_ref,
    rt_ref,
    bh_ref,
    bl_ref,
    out_ref,
    last_ref,
    xs,
    xr,
    ys,
    yr,
    hs,
    hr,
    acc,
    xs_sem,
    xr_sem,
    ys_sem,
    yr_sem,
    hs_sem,
    hr_sem,
    out_sem,
):
    me = lax.axis_index("mom")
    band = lax.axis_index("space")
    up, down = lax.rem(band + 1, bands), lax.rem(band + bands - 1, bands)
    half = points // 2
    size = plane_rows * ROWS
    part = peers * ROWS
    block = 8
    order = sorted(range(1, peers), key=lambda o: abs(2 * o - peers))

    barrier = pltpu.get_barrier_semaphore()
    for o in range(1, peers):
        pl.semaphore_signal(
            barrier, inc=1, device_id={"mom": lax.rem(me + o, peers)}, device_id_type=pl.DeviceIdType.MESH
        )
    for side in (up, down):
        pl.semaphore_signal(barrier, inc=1, device_id={"space": side}, device_id_type=pl.DeviceIdType.MESH)
    pl.semaphore_wait(barrier, peers + 1)

    def rows_of(peer):
        return pl.ds(pl.multiple_of(peer * size, 8), size)

    def x_copy(c, o):
        peer = lax.rem(me + o, peers)
        return pltpu.make_async_remote_copy(
            src_ref=xs.at[c, rows_of(peer)],
            dst_ref=xr.at[c, rows_of(me)],
            send_sem=xs_sem.at[c, o],
            recv_sem=xr_sem.at[c, o],
            device_id={"mom": peer},
            device_id_type=pl.DeviceIdType.MESH,
        )

    def x_own(c):
        return pltpu.make_async_copy(xs.at[c, rows_of(me)], xr.at[c, rows_of(me)], xs_sem.at[c, 0])

    def y_place(c, last):
        return last_ref.at[rows_of(me)] if last else yr.at[c, rows_of(me)]

    def y_copy(c, o, last):
        peer = lax.rem(me + o, peers)
        return pltpu.make_async_remote_copy(
            src_ref=ys.at[c, rows_of(peer)],
            dst_ref=y_place(c, last),
            send_sem=ys_sem.at[c, o],
            recv_sem=yr_sem.at[c, o],
            device_id={"mom": peer},
            device_id_type=pl.DeviceIdType.MESH,
        )

    def y_own(c, last):
        return pltpu.make_async_copy(ys.at[c, rows_of(me)], y_place(c, last), ys_sem.at[c, 0])

    def side_copy(which, side):
        return pltpu.make_async_remote_copy(
            src_ref=hs.at[which],
            dst_ref=hr.at[which],
            send_sem=hs_sem.at[which],
            recv_sem=hr_sem.at[which],
            device_id={"space": side},
            device_id_type=pl.DeviceIdType.MESH,
        )

    def forward(c, carry):
        taken = pl.ds(pl.multiple_of(c * part, 16), part)

        def planes(g, inner):
            wh, wl = wh_ref[taken, :], wl_ref[taken, :]
            for a in range(block):
                k = g * block + a
                y = left_product(wh, wl, x_ref[k])
                for d in range(peers):
                    at = pl.multiple_of((d * plane_rows + k) * ROWS, 8)
                    xs[c, pl.ds(at, ROWS), :] = y[d * ROWS : (d + 1) * ROWS]
            return inner

        lax.fori_loop(0, plane_rows // block, planes, 0)
        for o in order:
            x_copy(c, o).start()
        x_own(c).start()
        return carry

    lax.fori_loop(0, chunks, forward, 0)

    lane = lax.broadcasted_iota(jnp.int32, (half, cells), 1)

    def pack(k, carry):
        x = x_ref[k]
        top, bottom = x[:half], x[half:]
        at = pl.ds(pl.multiple_of(k * half, 8), half)
        hs[0, at, :] = jnp.where(lane < cells // 2, pltpu.roll(top, cells // 2, 1), bottom)
        hs[1, at, :] = jnp.where(lane < cells // 2, top, pltpu.roll(bottom, cells // 2, 1))
        return carry

    lax.fori_loop(0, plane_rows, pack, 0)
    side_copy(0, up).start()
    side_copy(1, down).start()

    row = lax.broadcasted_iota(jnp.int32, (points, 2 * cells), 0)
    speed = (2 * row - (points - 1)).astype(F32) * (FRICTION / points)
    cell_row = lax.broadcasted_iota(jnp.int32, (points, cells), 0)
    signed = jnp.where(cell_row < half, cell_row, cell_row - points)
    squares = signed * signed
    exact = dict(precision=lax.Precision.HIGHEST, preferred_element_type=F32)
    scale = DAMPING / (half * half)

    def middle(c, last):
        for o in order:
            x_copy(c, o).wait_recv()
        x_own(c).wait()
        for i in range(PER):
            mode = me * (chunks * PER) + c * PER + i
            re = xr[c, pl.ds(2 * i, points, stride=ROWS), :]
            im = xr[c, pl.ds(2 * i + 1, points, stride=ROWS), :]
            x = jnp.concatenate([re, im], axis=1)
            pq = left_product(th_ref[...], tl_ref[...], x)
            pr, pi = pq[:points, :cells], pq[:points, cells:]
            qr, qi = pq[points:, :cells], pq[points:, cells:]
            s = jnp.dot(a_ref[...], b_ref[c * PER + i], **exact)
            d = scale * (squares + mode * mode).astype(F32)
            xre, xim = pr + qi, pi - qr
            ur = -d * xre - s * xim
            ui = s * xre - d * xim
            vr, vi = -ui, ur
            if i == 0:
                end = jnp.dot(a_ref[...], b_ref[chunks * PER], **exact)
                de = scale * (squares + half * half).astype(F32)
                real = mode == 0
                ur = jnp.where(real, s * qr - d * pr, ur)
                ui = jnp.where(real, end * qi - de * pi, ui)
                vr = jnp.where(real, -d * qr - s * pr, vr)
                vi = jnp.where(real, -de * qi - end * pi, vi)
            uv = jnp.concatenate(
                [jnp.concatenate([ur, ui], axis=1), jnp.concatenate([vr, vi], axis=1)], axis=0
            )
            y = left_product(ih_ref[...], il_ref[...], uv) + difference(speed * x, row, points)
            ys[c, pl.ds(2 * i, points, stride=ROWS), :] = y[:, :cells]
            ys[c, pl.ds(2 * i + 1, points, stride=ROWS), :] = y[:, cells:]
        for o in order:
            y_copy(c, o, last).start()
        y_own(c, last).start()

    def middle_step(c, carry):
        middle(c, False)
        return carry

    if chunks > 1:
        lax.fori_loop(0, chunks - 1, middle_step, 0)
    middle(chunks - 1, True)

    side_copy(0, up).wait_recv()
    side_copy(1, down).wait_recv()
    cell_speed = (2 * cell_row - (points - 1)).astype(F32) / points

    def advect(g, carry):
        for a in range(block):
            k = g * block + a
            x = x_ref[k]
            at = pl.ds(pl.multiple_of(k * half, 8), half)
            top = exact_product(x[:half], plus_ref[...])
            bottom = exact_product(x[half:], minus_ref[...])
            sides = exact_product(hr[0, at, :], lt_ref[...]) + exact_product(hr[1, at, :], rt_ref[...])
            rows = jnp.concatenate(
                [top[:, :cells] + sides[:, :cells], bottom[:, :cells] + sides[:, cells:]], 0
            )
            columns = jnp.concatenate([top[:, cells:], bottom[:, cells:]], 0)
            first = (2 * (me * plane_rows + k) - (points - 1)).astype(F32) * (1.0 / points)
            acc[k] = FRICTION * difference(cell_speed * x, cell_row, points) - (
                first * rows + cell_speed * columns
            ) * (1.0 / 60.0)
        return carry

    lax.fori_loop(0, plane_rows // block, advect, 0)

    def gather(c, carry):
        for o in order:
            y_copy(c, o, False).wait_recv()
        y_own(c, False).wait()

        def planes(g, inner):
            for a in range(block):
                k = g * block + a
                y = jnp.concatenate(
                    [
                        yr[c, pl.ds(pl.multiple_of((d * plane_rows + k) * ROWS, 8), ROWS), :]
                        for d in range(peers)
                    ],
                    axis=0,
                )
                acc[k] += left_product(bh_ref[c], bl_ref[c], y)
            return inner

        lax.fori_loop(0, plane_rows // block, planes, 0)
        return carry

    if chunks > 1:
        lax.fori_loop(0, chunks - 1, gather, 0)
    out = pltpu.make_async_copy(acc, out_ref, out_sem)
    out.start()

    def sent(c, carry):
        for o in order:
            x_copy(c, o).wait_send()
        return carry

    def sent_back(c, carry):
        for o in order:
            y_copy(c, o, False).wait_send()
        return carry

    lax.fori_loop(0, chunks, sent, 0)
    if chunks > 1:
        lax.fori_loop(0, chunks - 1, sent_back, 0)
    side_copy(0, up).wait_send()
    side_copy(1, down).wait_send()
    out.wait()
    for o in order:
        y_copy(chunks - 1, o, True).wait()
    y_own(chunks - 1, True).wait()


def back_kernel(peers, block, base_ref, wh_ref, wl_ref, y_ref, o_ref):
    for a in range(block):
        y = jnp.concatenate([y_ref[d, a] for d in range(peers)], axis=0)
        o_ref[a] = base_ref[a] + left_product(wh_ref[...], wl_ref[...], y)


def whole(shape):
    return pl.BlockSpec(shape, lambda *_: (0,) * len(shape))


def params(mib=48):
    return pltpu.CompilerParams(vmem_limit_bytes=mib * 2**20)


def cost(flops, size):
    return pl.CostEstimate(flops=int(flops), bytes_accessed=int(size), transcendentals=0)


def local(density, mode_waves, mode_amplitudes, mode_phases):
    plane_rows, points, cells = density.shape
    rows_dev = cells // NY
    peers = lax.axis_size("mom")
    bands = lax.axis_size("space")
    total_rows = rows_dev * bands
    mom = lax.axis_index("mom")
    space = lax.axis_index("space")
    per_peer = points // 2 // peers
    chunks = per_peer // PER
    block = 8
    steps = plane_rows // block
    half = points // 2
    size = plane_rows * points * cells * 4

    forward, back = second_tables(points, peers)
    part = peers * ROWS
    wh, wl = halves(forward)
    bh, bl = halves(np.stack([back[:, c * part : (c + 1) * part] for c in range(chunks)]))
    first, inverse = first_tables(points)
    th, tl = halves(first)
    ih, il = halves(inverse)

    index = jnp.arange(points, dtype=jnp.int32)
    signed = jnp.where(index < half, index, index - points)
    unit = np.float32(np.pi / points)
    a_angle = unit * (mode_waves[None, :, 0] * signed[:, None] % (2 * points)).astype(F32)
    a_sine = jnp.where(index[:, None] == half, 0.0, jnp.sin(a_angle))
    a_table = jnp.concatenate([a_sine, jnp.cos(a_angle)], axis=1)
    cell = jnp.arange(cells, dtype=jnp.int32)
    turn_rows = mode_waves[:, 0:1] * (space * rows_dev + cell // NY)[None, :] % total_rows
    turn_columns = mode_waves[:, 1:2] * (cell % NY)[None, :] % NY
    angles = (
        2.0 * np.pi * (turn_rows.astype(F32) / total_rows + turn_columns.astype(F32) / NY)
        + mode_phases[:, None]
    )
    cell_factor = mode_amplitudes[:, None] * jnp.sin(angles)

    def mode_factors(modes):
        b_angle = unit * (mode_waves[None, :, 1] * modes[:, None] % (2 * points)).astype(F32)
        waves = jnp.concatenate([jnp.cos(b_angle), jnp.sin(b_angle)], axis=1)
        return waves[:, :, None] * jnp.concatenate([cell_factor, cell_factor], axis=0)[None]

    modes = mom * per_peer + jnp.arange(per_peer, dtype=jnp.int32)
    b_table = mode_factors(jnp.concatenate([modes, jnp.full((1,), -half, jnp.int32)]))

    positive = mom * plane_rows >= half
    own_m, left_m, right_m = row_tables(cells, MINUS)
    own_p, left_p, right_p = row_tables(cells, PLUS)

    def chosen(minus, plus):
        return jnp.where(positive, jnp.asarray(minus, BF16), jnp.asarray(plus, BF16))

    def beside(columns):
        return chosen(np.concatenate([own_m, columns], 1), np.concatenate([own_p, columns], 1))

    vm = pl.BlockSpec(memory_space=pltpu.VMEM)
    anywhere = pl.BlockSpec(memory_space=pl.ANY)
    message_rows = peers * plane_rows * ROWS
    chunked = pltpu.VMEM((chunks, message_rows, cells), F32)
    sides = pltpu.VMEM((2, plane_rows * half, cells), F32)
    flags = pltpu.SemaphoreType.DMA((chunks, peers))
    pair = pltpu.SemaphoreType.DMA((2,))
    base, last = pl.pallas_call(
        functools.partial(exchange_kernel, peers, bands, chunks, plane_rows, points, cells),
        out_shape=[
            jax.ShapeDtypeStruct(density.shape, F32),
            jax.ShapeDtypeStruct((message_rows, cells), F32),
        ],
        in_specs=[vm] * 15,
        out_specs=[anywhere] * 2,
        scratch_shapes=[chunked] * 4
        + [sides] * 2
        + [pltpu.VMEM(density.shape, F32)]
        + [flags] * 4
        + [pair] * 2
        + [pltpu.SemaphoreType.DMA],
        compiler_params=pltpu.CompilerParams(
            vmem_limit_bytes=56 * 2**20, collective_id=0, has_side_effects=True
        ),
        cost_estimate=cost(3 * 3.2e9, 3 * size),
        name="exchange",
    )(
        density,
        wh,
        wl,
        th,
        tl,
        ih,
        il,
        a_table,
        b_table,
        beside(column_table(cells, PLUS)),
        beside(column_table(cells, MINUS)),
        chosen(left_m, left_p),
        chosen(right_m, right_p),
        bh,
        bl,
    )
    plane = lambda g: (g, 0, 0)
    return pl.pallas_call(
        functools.partial(back_kernel, peers, block),
        grid=(steps,),
        out_shape=jax.ShapeDtypeStruct(density.shape, F32),
        in_specs=[
            pl.BlockSpec((block, points, cells), plane),
            whole(bh.shape[1:]),
            whole(bl.shape[1:]),
            pl.BlockSpec((peers, block, ROWS, cells), lambda g: (0, g, 0, 0)),
        ],
        out_specs=pl.BlockSpec((block, points, cells), plane),
        compiler_params=params(),
        cost_estimate=cost(6 * plane_rows * points * part * cells, 3 * size),
        name="second_inverse",
    )(base, bh[-1], bl[-1], last.reshape(peers, plane_rows, ROWS, cells))


def solution(mesh):
    return jax.shard_map(
        local,
        mesh=mesh,
        in_specs=(P("mom", None, "space"), P(), P(), P()),
        out_specs=P("mom", None, "space"),
        check_vma=False,
    )
```

```python
import functools

import jax
import jax.numpy as jnp
import ml_dtypes
import numpy as np
from jax import lax
from jax.experimental import pallas as pl
from jax.experimental.pallas import tpu as pltpu
from jax.sharding import PartitionSpec as P

NY = 16
PER = 4
ROWS = 2 * PER
DAMPING = 0.5
FRICTION = 0.5
BF16 = jnp.bfloat16
F32 = jnp.float32
MINUS = ((-3, -2.0), (-2, 15.0), (-1, -60.0), (0, 20.0), (1, 30.0), (2, -3.0))
PLUS = ((3, 2.0), (2, -15.0), (1, 60.0), (0, -20.0), (-1, -30.0), (-2, 3.0))


def halves(table):
    high = table.astype(ml_dtypes.bfloat16)
    low = (table - high.astype(np.float64)).astype(ml_dtypes.bfloat16)
    return jnp.asarray(high), jnp.asarray(low)


def mode_order(points, peers):
    per_peer = points // 2 // peers
    return [
        d * per_peer + c * PER + i
        for c in range(per_peer // PER)
        for d in range(peers)
        for i in range(PER)
    ]


def second_tables(points, peers):
    k = np.arange(points)
    forward, back = [], []
    for m in mode_order(points, peers):
        angle = 2.0 * np.pi / points * (k * m % points)
        if m == 0:
            sign = 1.0 - 2.0 * (k % 2)
            forward += [np.ones(points), sign]
            back += [np.ones(points) / points, sign / points]
        else:
            forward += [np.cos(angle), -np.sin(angle)]
            back += [2.0 / points * np.cos(angle), -2.0 / points * np.sin(angle)]
    return np.stack(forward), np.stack(back).T.copy()


def first_tables(points):
    k = np.arange(points)
    turned = k[:, None] * k[None, :] % points
    cosine = np.cos(2.0 * np.pi / points * turned)
    sine = np.sin(2.0 * np.pi / points * turned)
    sine[turned * 2 % points == 0] = 0.0
    return np.concatenate([cosine, sine], 0), np.concatenate([cosine, sine], 1) / points


def row_tables(cells, stencil):
    own = np.zeros((cells, cells))
    left = np.zeros((2, cells, cells))
    right = np.zeros((2, cells, cells))
    half = cells // 2
    for n in range(cells):
        for s, w in stencil:
            src = n + s * NY
            if src < 0:
                for h in range(2):
                    left[h, src + half + h * half, n] += w
            elif src >= cells:
                for h in range(2):
                    right[h, src - cells + h * half, n] += w
            else:
                own[src, n] += w
    return own, np.concatenate(list(left), 1), np.concatenate(list(right), 1)


def column_table(cells, stencil):
    table = np.zeros((cells, cells))
    for n in range(cells):
        for s, w in stencil:
            table[n // NY * NY + (n % NY + s) % NY, n] += w
    return table


def split(value):
    high = value.astype(BF16)
    return high, (value - high.astype(F32)).astype(BF16)


def mm(a, b):
    return jnp.dot(a, b, preferred_element_type=F32)


def left_product(high, low, value):
    vh, vl = split(value)
    return mm(high, vh) + (mm(high, vl) + mm(low, vh))


def exact_product(value, table):
    vh, vl = split(value)
    return mm(vh, table) + mm(vl, table)


def difference(weighted, row, points):
    above = jnp.where(row < points - 1, pltpu.roll(weighted, points - 1, 0), 0.0)
    below = jnp.where(row > 0, pltpu.roll(weighted, 1, 0), 0.0)
    return above - below


def exchange_kernel(
    peers,
    bands,
    chunks,
    plane_rows,
    points,
    cells,
    source_ref,
    wh_ref,
    wl_ref,
    th_ref,
    tl_ref,
    ih_ref,
    il_ref,
    waves_ref,
    amp_ref,
    phase_ref,
    plus_ref,
    minus_ref,
    lt_ref,
    rt_ref,
    bh_ref,
    bl_ref,
    out_ref,
    last_ref,
    xs,
    xr,
    ys,
    yr,
    hs,
    hr,
    acc,
    x_ref,
    a_ref,
    cf_ref,
    xs_sem,
    xr_sem,
    ys_sem,
    yr_sem,
    hs_sem,
    hr_sem,
    out_sem,
    in_sem,
):
    me = lax.axis_index("mom")
    band = lax.axis_index("space")
    up, down = lax.rem(band + 1, bands), lax.rem(band + bands - 1, bands)
    half = points // 2
    size = plane_rows * ROWS
    part = peers * ROWS
    block = 8
    groups = plane_rows // block
    side = peers // 2
    mine = me // side * side
    far = side - mine
    order = [far + lax.rem(me + j, side) for j in range(side)]
    order += [mine + lax.rem(me + j, side) for j in range(1, side)]

    def load(g):
        planes = pl.ds(pl.multiple_of(g * block, block), block)
        return pltpu.make_async_copy(source_ref.at[planes], x_ref.at[planes], in_sem.at[g])

    for g in range(groups):
        load(g).start()

    barrier = pltpu.get_barrier_semaphore()
    for o in range(1, peers):
        pl.semaphore_signal(
            barrier, inc=1, device_id={"mom": lax.rem(me + o, peers)}, device_id_type=pl.DeviceIdType.MESH
        )
    for side in (up, down):
        pl.semaphore_signal(barrier, inc=1, device_id={"space": side}, device_id_type=pl.DeviceIdType.MESH)

    def rows_of(peer):
        return pl.ds(pl.multiple_of(peer * size, 8), size)

    def x_copy(c, peer, source=me):
        return pltpu.make_async_remote_copy(
            src_ref=xs.at[c, rows_of(peer)],
            dst_ref=xr.at[c, rows_of(me)],
            send_sem=xs_sem.at[c, peer],
            recv_sem=xr_sem.at[c, source],
            device_id={"mom": peer},
            device_id_type=pl.DeviceIdType.MESH,
        )

    def x_own(c):
        return pltpu.make_async_copy(xs.at[c, rows_of(me)], xr.at[c, rows_of(me)], xs_sem.at[c, me])

    def y_place(c, last):
        return last_ref.at[rows_of(me)] if last else yr.at[c, rows_of(me)]

    def y_copy(c, peer, last, source=me):
        return pltpu.make_async_remote_copy(
            src_ref=ys.at[c, rows_of(peer)],
            dst_ref=y_place(c, last),
            send_sem=ys_sem.at[c, peer],
            recv_sem=yr_sem.at[c, source],
            device_id={"mom": peer},
            device_id_type=pl.DeviceIdType.MESH,
        )

    def y_own(c, last):
        return pltpu.make_async_copy(ys.at[c, rows_of(me)], y_place(c, last), ys_sem.at[c, me])

    def side_copy(which, side):
        return pltpu.make_async_remote_copy(
            src_ref=hs.at[which],
            dst_ref=hr.at[which],
            send_sem=hs_sem.at[which],
            recv_sem=hr_sem.at[which],
            device_id={"space": side},
            device_id_type=pl.DeviceIdType.MESH,
        )

    def transform(c, loading):
        taken = pl.ds(pl.multiple_of(c * part, 16), part)

        def planes(g, inner):
            if loading:
                load(g).wait()
            wh, wl = wh_ref[taken, :], wl_ref[taken, :]
            for a in range(block):
                k = g * block + a
                y = left_product(wh, wl, x_ref[k])
                for d in range(peers):
                    at = pl.multiple_of((d * plane_rows + k) * ROWS, 8)
                    xs[c, pl.ds(at, ROWS), :] = y[d * ROWS : (d + 1) * ROWS]
            return inner

        lax.fori_loop(0, groups, planes, 0)

    def send(c):
        for o in order:
            x_copy(c, o).start()
        x_own(c).start()

    def forward(c, carry):
        transform(c, False)
        send(c)
        return carry

    transform(0, True)
    pl.semaphore_wait(barrier, peers + 1)
    send(0)
    if chunks > 1:
        lax.fori_loop(1, chunks, forward, 0)

    lane = lax.broadcasted_iota(jnp.int32, (half, cells), 1)

    def pack(k, carry):
        x = x_ref[k]
        top, bottom = x[:half], x[half:]
        at = pl.ds(pl.multiple_of(k * half, 8), half)
        hs[0, at, :] = jnp.where(lane < cells // 2, pltpu.roll(top, cells // 2, 1), bottom)
        hs[1, at, :] = jnp.where(lane < cells // 2, top, pltpu.roll(bottom, cells // 2, 1))
        return carry

    lax.fori_loop(0, plane_rows, pack, 0)
    side_copy(0, up).start()
    side_copy(1, down).start()

    row = lax.broadcasted_iota(jnp.int32, (points, 2 * cells), 0)
    speed = (2 * row - (points - 1)).astype(F32) * (FRICTION / points)
    cell_row = lax.broadcasted_iota(jnp.int32, (points, cells), 0)
    signed = jnp.where(cell_row < half, cell_row, cell_row - points)
    squares = signed * signed
    exact = dict(precision=lax.Precision.HIGHEST, preferred_element_type=F32)
    scale = DAMPING / (half * half)


    modes = waves_ref.shape[0]
    waves = waves_ref[...].astype(F32)
    w_row, w_column = waves[:, 0:1], waves[:, 1:2]
    eye = lax.broadcasted_iota(jnp.int32, (modes, modes), 0) == lax.broadcasted_iota(
        jnp.int32, (modes, modes), 1
    )

    def upright(value):
        return jnp.sum(jnp.where(eye, jnp.broadcast_to(value, (modes, modes)), 0.0), axis=1, keepdims=True)

    def turned(value, period):
        return value - period * jnp.floor(value / period)

    unit = np.float32(np.pi / points)
    freq = lax.broadcasted_iota(jnp.int32, (modes, points), 1)
    freq_signed = jnp.where(freq < half, freq, freq - points).astype(F32)
    a_angle = unit * turned(w_row * freq_signed, 2.0 * points)
    a_ref[:modes] = jnp.where(freq == half, 0.0, jnp.sin(a_angle))
    a_ref[modes:] = jnp.cos(a_angle)
    rows_dev = cells // NY
    cell = lax.broadcasted_iota(jnp.int32, (modes, cells), 1).astype(F32)
    cell_line = jnp.floor(cell / NY)
    cell_column = cell - NY * cell_line
    cell_line = cell_line + (band * rows_dev).astype(F32)
    total_rows = float(rows_dev * bands)
    angles = (
        2.0 * np.pi * (turned(w_row * cell_line, total_rows) / total_rows + turned(w_column * cell_column, float(NY)) / NY)
        + upright(phase_ref[...])
    )
    cf_ref[...] = upright(amp_ref[...]) * jnp.sin(angles)

    def symbol(mode):
        b_angle = unit * turned(w_column * jnp.full((modes, cells), mode, jnp.int32).astype(F32), 2.0 * points)
        factor = jnp.concatenate([jnp.cos(b_angle) * cf_ref[...], jnp.sin(b_angle) * cf_ref[...]], axis=0)
        return lax.dot_general(a_ref[...], factor, (((0,), (0,)), ((), ())), **exact)

    def middle(c, last):
        for o in order:
            x_copy(c, o, o).wait_recv()
        x_own(c).wait()
        for i in range(PER):
            mode = me * (chunks * PER) + c * PER + i
            re = xr[c, pl.ds(2 * i, points, stride=ROWS), :]
            im = xr[c, pl.ds(2 * i + 1, points, stride=ROWS), :]
            x = jnp.concatenate([re, im], axis=1)
            pq = left_product(th_ref[...], tl_ref[...], x)
            pr, pi = pq[:points, :cells], pq[:points, cells:]
            qr, qi = pq[points:, :cells], pq[points:, cells:]
            s = symbol(mode)
            d = scale * (squares + mode * mode).astype(F32)
            xre, xim = pr + qi, pi - qr
            ur = -d * xre - s * xim
            ui = s * xre - d * xim
            vr, vi = -ui, ur
            if i == 0:
                end = symbol(-half)
                de = scale * (squares + half * half).astype(F32)
                real = mode == 0
                ur = jnp.where(real, s * qr - d * pr, ur)
                ui = jnp.where(real, end * qi - de * pi, ui)
                vr = jnp.where(real, -d * qr - s * pr, vr)
                vi = jnp.where(real, -de * qi - end * pi, vi)
            uv = jnp.concatenate(
                [jnp.concatenate([ur, ui], axis=1), jnp.concatenate([vr, vi], axis=1)], axis=0
            )
            y = left_product(ih_ref[...], il_ref[...], uv) + difference(speed * x, row, points)
            ys[c, pl.ds(2 * i, points, stride=ROWS), :] = y[:, :cells]
            ys[c, pl.ds(2 * i + 1, points, stride=ROWS), :] = y[:, cells:]
        for o in order:
            y_copy(c, o, last).start()
        y_own(c, last).start()

    def middle_step(c, carry):
        middle(c, False)
        return carry

    if chunks > 1:
        lax.fori_loop(0, chunks - 1, middle_step, 0)
    middle(chunks - 1, True)

    side_copy(0, up).wait_recv()
    side_copy(1, down).wait_recv()
    stencil = me * plane_rows // half
    cell_speed = (2 * cell_row - (points - 1)).astype(F32) / points

    def advect(g, carry):
        for a in range(block):
            k = g * block + a
            x = x_ref[k]
            at = pl.ds(pl.multiple_of(k * half, 8), half)
            top = exact_product(x[:half], plus_ref[stencil])
            bottom = exact_product(x[half:], minus_ref[stencil])
            sides = exact_product(hr[0, at, :], lt_ref[stencil]) + exact_product(hr[1, at, :], rt_ref[stencil])
            rows = jnp.concatenate(
                [top[:, :cells] + sides[:, :cells], bottom[:, :cells] + sides[:, cells:]], 0
            )
            columns = jnp.concatenate([top[:, cells:], bottom[:, cells:]], 0)
            first = (2 * (me * plane_rows + k) - (points - 1)).astype(F32) * (1.0 / points)
            acc[k] = FRICTION * difference(cell_speed * x, cell_row, points) - (
                first * rows + cell_speed * columns
            ) * (1.0 / 60.0)
        return carry

    lax.fori_loop(0, plane_rows // block, advect, 0)

    def gather(c, carry):
        for o in order:
            y_copy(c, o, False, o).wait_recv()
        y_own(c, False).wait()

        def planes(g, inner):
            for a in range(block):
                k = g * block + a
                y = jnp.concatenate(
                    [
                        yr[c, pl.ds(pl.multiple_of((d * plane_rows + k) * ROWS, 8), ROWS), :]
                        for d in range(peers)
                    ],
                    axis=0,
                )
                acc[k] += left_product(bh_ref[c], bl_ref[c], y)
            return inner

        lax.fori_loop(0, plane_rows // block, planes, 0)
        return carry

    if chunks > 1:
        lax.fori_loop(0, chunks - 1, gather, 0)
    out = pltpu.make_async_copy(acc, out_ref, out_sem)
    out.start()

    def sent(c, carry):
        for o in order:
            x_copy(c, o).wait_send()
        return carry

    def sent_back(c, carry):
        for o in order:
            y_copy(c, o, False).wait_send()
        return carry

    lax.fori_loop(0, chunks, sent, 0)
    if chunks > 1:
        lax.fori_loop(0, chunks - 1, sent_back, 0)
    side_copy(0, up).wait_send()
    side_copy(1, down).wait_send()
    out.wait()
    for o in order:
        y_copy(chunks - 1, o, True).wait_send()
    for o in order:
        y_copy(chunks - 1, o, True, o).wait_recv()
    y_own(chunks - 1, True).wait()


def back_kernel(peers, block, base_ref, wh_ref, wl_ref, y_ref, o_ref):
    for a in range(block):
        y = jnp.concatenate([y_ref[d, a] for d in range(peers)], axis=0)
        o_ref[a] = base_ref[a] + left_product(wh_ref[...], wl_ref[...], y)


def whole(shape):
    return pl.BlockSpec(shape, lambda *_: (0,) * len(shape))


def params(mib=48):
    return pltpu.CompilerParams(vmem_limit_bytes=mib * 2**20)


def cost(flops, size):
    return pl.CostEstimate(flops=int(flops), bytes_accessed=int(size), transcendentals=0)


def local(density, mode_waves, mode_amplitudes, mode_phases):
    plane_rows, points, cells = density.shape
    peers = lax.axis_size("mom")
    bands = lax.axis_size("space")
    per_peer = points // 2 // peers
    chunks = per_peer // PER
    block = 8
    steps = plane_rows // block
    half = points // 2
    size = plane_rows * points * cells * 4

    forward, back = second_tables(points, peers)
    part = peers * ROWS
    wh, wl = halves(forward)
    bh, bl = halves(np.stack([back[:, c * part : (c + 1) * part] for c in range(chunks)]))
    first, inverse = first_tables(points)
    th, tl = halves(first)
    ih, il = halves(inverse)

    own_m, left_m, right_m = row_tables(cells, MINUS)
    own_p, left_p, right_p = row_tables(cells, PLUS)

    def chosen(minus, plus):
        return jnp.asarray(np.stack([plus, minus]).astype(ml_dtypes.bfloat16))

    def beside(columns):
        return chosen(np.concatenate([own_m, columns], 1), np.concatenate([own_p, columns], 1))

    vm = pl.BlockSpec(memory_space=pltpu.VMEM)
    anywhere = pl.BlockSpec(memory_space=pl.ANY)
    message_rows = peers * plane_rows * ROWS
    chunked = pltpu.VMEM((chunks, message_rows, cells), F32)
    sides = pltpu.VMEM((2, plane_rows * half, cells), F32)
    flags = pltpu.SemaphoreType.DMA((chunks, peers))
    pair = pltpu.SemaphoreType.DMA((2,))
    base, last = pl.pallas_call(
        functools.partial(exchange_kernel, peers, bands, chunks, plane_rows, points, cells),
        out_shape=[
            jax.ShapeDtypeStruct(density.shape, F32),
            jax.ShapeDtypeStruct((message_rows, cells), F32),
        ],
        in_specs=[anywhere] + [vm] * 15,
        out_specs=[anywhere] * 2,
        scratch_shapes=[chunked] * 4
        + [sides] * 2
        + [pltpu.VMEM(density.shape, F32)] * 2
        + [pltpu.VMEM((2 * mode_waves.shape[0], points), F32)]
        + [pltpu.VMEM((mode_waves.shape[0], cells), F32)]
        + [flags] * 4
        + [pair] * 2
        + [pltpu.SemaphoreType.DMA, pltpu.SemaphoreType.DMA((steps,))],
        compiler_params=pltpu.CompilerParams(
            vmem_limit_bytes=56 * 2**20, collective_id=0, has_side_effects=True
        ),
        cost_estimate=cost(3 * 3.2e9, 3 * size),
        name="exchange",
    )(
        density,
        wh,
        wl,
        th,
        tl,
        ih,
        il,
        mode_waves,
        mode_amplitudes.reshape(1, -1),
        mode_phases.reshape(1, -1),
        beside(column_table(cells, PLUS)),
        beside(column_table(cells, MINUS)),
        chosen(left_m, left_p),
        chosen(right_m, right_p),
        bh,
        bl,
    )
    plane = lambda g: (g, 0, 0)
    return pl.pallas_call(
        functools.partial(back_kernel, peers, block),
        grid=(steps,),
        out_shape=jax.ShapeDtypeStruct(density.shape, F32),
        in_specs=[
            pl.BlockSpec((block, points, cells), plane),
            whole(bh.shape[1:]),
            whole(bl.shape[1:]),
            pl.BlockSpec((peers, block, ROWS, cells), lambda g: (0, g, 0, 0)),
        ],
        out_specs=pl.BlockSpec((block, points, cells), plane),
        compiler_params=params(60),
        cost_estimate=cost(6 * plane_rows * points * part * cells, 3 * size),
        name="second_inverse",
    )(base, bh[-1], bl[-1], last.reshape(peers, plane_rows, ROWS, cells))


def solution(mesh):
    return jax.shard_map(
        local,
        mesh=mesh,
        in_specs=(P("mom", None, "space"), P(), P(), P()),
        out_specs=P("mom", None, "space"),
        check_vma=False,
    )
```

```python
import functools

import jax
import jax.numpy as jnp
import ml_dtypes
import numpy as np
from jax import lax
from jax.experimental import pallas as pl
from jax.experimental.pallas import tpu as pltpu
from jax.sharding import PartitionSpec as P

NY = 16
PER = 4
ROWS = 2 * PER
DAMPING = 0.5
FRICTION = 0.5
BF16 = jnp.bfloat16
F32 = jnp.float32
MINUS = ((-3, -2.0), (-2, 15.0), (-1, -60.0), (0, 20.0), (1, 30.0), (2, -3.0))
PLUS = ((3, 2.0), (2, -15.0), (1, 60.0), (0, -20.0), (-1, -30.0), (-2, 3.0))


def halves(table):
    high = table.astype(ml_dtypes.bfloat16)
    low = (table - high.astype(np.float64)).astype(ml_dtypes.bfloat16)
    return high, low


def mode_order(points, peers):
    per_peer = points // 2 // peers
    return [
        d * per_peer + c * PER + i
        for c in range(per_peer // PER)
        for d in range(peers)
        for i in range(PER)
    ]


def second_tables(points, peers):
    k = np.arange(points)
    forward, back = [], []
    for m in mode_order(points, peers):
        angle = 2.0 * np.pi / points * (k * m % points)
        if m == 0:
            sign = 1.0 - 2.0 * (k % 2)
            forward += [np.ones(points), sign]
            back += [np.ones(points) / points, sign / points]
        else:
            forward += [np.cos(angle), -np.sin(angle)]
            back += [2.0 / points * np.cos(angle), -2.0 / points * np.sin(angle)]
    return np.stack(forward), np.stack(back).T.copy()


def first_tables(points):
    k = np.arange(points)
    turned = k[:, None] * k[None, :] % points
    cosine = np.cos(2.0 * np.pi / points * turned)
    sine = np.sin(2.0 * np.pi / points * turned)
    sine[turned * 2 % points == 0] = 0.0
    return np.concatenate([cosine, sine], 0), np.concatenate([cosine, sine], 1) / points


def row_tables(cells, stencil):
    own = np.zeros((cells, cells))
    left = np.zeros((2, cells, cells))
    right = np.zeros((2, cells, cells))
    half = cells // 2
    for n in range(cells):
        for s, w in stencil:
            src = n + s * NY
            if src < 0:
                for h in range(2):
                    left[h, src + half + h * half, n] += w
            elif src >= cells:
                for h in range(2):
                    right[h, src - cells + h * half, n] += w
            else:
                own[src, n] += w
    return own, np.concatenate(list(left), 1), np.concatenate(list(right), 1)


def column_table(cells, stencil):
    table = np.zeros((cells, cells))
    for n in range(cells):
        for s, w in stencil:
            table[n // NY * NY + (n % NY + s) % NY, n] += w
    return table


def split(value):
    high = value.astype(BF16)
    return high, (value - high.astype(F32)).astype(BF16)


def mm(a, b):
    return jnp.dot(a, b, preferred_element_type=F32)


def left_product(high, low, value):
    vh, vl = split(value)
    return mm(high, vh) + (mm(high, vl) + mm(low, vh))


def exact_product(value, table):
    vh, vl = split(value)
    return mm(vh, table) + mm(vl, table)


def stacked_product(table, value):
    vh, vl = split(value)
    return mm(table, jnp.concatenate([vh, vh, vl], axis=0))


def difference(weighted, row, points):
    above = jnp.where(row < points - 1, pltpu.roll(weighted, points - 1, 0), 0.0)
    below = jnp.where(row > 0, pltpu.roll(weighted, 1, 0), 0.0)
    return above - below


def exchange_kernel(
    peers,
    bands,
    chunks,
    plane_rows,
    points,
    cells,
    source_ref,
    wh_ref,
    wl_ref,
    th_ref,
    tl_ref,
    ih_ref,
    il_ref,
    waves_ref,
    amp_ref,
    phase_ref,
    plus_ref,
    minus_ref,
    lt_ref,
    rt_ref,
    bs_ref,
    out_ref,
    last_ref,
    xs,
    xr,
    ys,
    yr,
    hs,
    hr,
    acc,
    x_ref,
    a_ref,
    cf_ref,
    xs_sem,
    xr_sem,
    ys_sem,
    yr_sem,
    hs_sem,
    hr_sem,
    out_sem,
    in_sem,
):
    me = lax.axis_index("mom")
    band = lax.axis_index("space")
    up, down = lax.rem(band + 1, bands), lax.rem(band + bands - 1, bands)
    half = points // 2
    size = plane_rows * ROWS
    part = peers * ROWS
    block = 8
    groups = plane_rows // block
    side = peers // 2
    mine = me // side * side
    far = side - mine
    order = [far + lax.rem(me + j, side) for j in range(side)]
    order += [mine + lax.rem(me + j, side) for j in range(1, side)]

    def load(g):
        planes = pl.ds(pl.multiple_of(g * block, block), block)
        return pltpu.make_async_copy(source_ref.at[planes], x_ref.at[planes], in_sem.at[g])

    for g in range(groups):
        load(g).start()

    barrier = pltpu.get_barrier_semaphore()
    for o in range(1, peers):
        pl.semaphore_signal(
            barrier, inc=1, device_id={"mom": lax.rem(me + o, peers)}, device_id_type=pl.DeviceIdType.MESH
        )
    for side in (up, down):
        pl.semaphore_signal(barrier, inc=1, device_id={"space": side}, device_id_type=pl.DeviceIdType.MESH)

    def rows_of(peer):
        return pl.ds(pl.multiple_of(peer * size, 8), size)

    def x_copy(c, peer, source=me):
        return pltpu.make_async_remote_copy(
            src_ref=xs.at[c, rows_of(peer)],
            dst_ref=xr.at[c, rows_of(me)],
            send_sem=xs_sem.at[c, peer],
            recv_sem=xr_sem.at[c, source],
            device_id={"mom": peer},
            device_id_type=pl.DeviceIdType.MESH,
        )

    def x_own(c):
        return pltpu.make_async_copy(xs.at[c, rows_of(me)], xr.at[c, rows_of(me)], xs_sem.at[c, me])

    def y_place(c, last):
        return last_ref.at[rows_of(me)] if last else yr.at[c, rows_of(me)]

    def y_copy(c, peer, last, source=me):
        return pltpu.make_async_remote_copy(
            src_ref=ys.at[c, rows_of(peer)],
            dst_ref=y_place(c, last),
            send_sem=ys_sem.at[c, peer],
            recv_sem=yr_sem.at[c, source],
            device_id={"mom": peer},
            device_id_type=pl.DeviceIdType.MESH,
        )

    def y_own(c, last):
        return pltpu.make_async_copy(ys.at[c, rows_of(me)], y_place(c, last), ys_sem.at[c, me])

    def side_copy(which, side):
        return pltpu.make_async_remote_copy(
            src_ref=hs.at[which],
            dst_ref=hr.at[which],
            send_sem=hs_sem.at[which],
            recv_sem=hr_sem.at[which],
            device_id={"space": side},
            device_id_type=pl.DeviceIdType.MESH,
        )

    def transform(c, loading):
        taken = pl.ds(pl.multiple_of(c * part, 16), part)

        def planes(g, inner):
            if loading:
                load(g).wait()
            wh, wl = wh_ref[taken, :], wl_ref[taken, :]
            for a in range(0, block, 2):
                k = g * block + a
                y = left_product(wh, wl, jnp.concatenate([x_ref[k], x_ref[k + 1]], axis=1))
                for d in range(peers):
                    at = pl.multiple_of((d * plane_rows + k) * ROWS, 8)
                    xs[c, pl.ds(at, ROWS), :] = y[d * ROWS : (d + 1) * ROWS, :cells]
                    xs[c, pl.ds(at + ROWS, ROWS), :] = y[d * ROWS : (d + 1) * ROWS, cells:]
            return inner

        lax.fori_loop(0, groups, planes, 0)

    def send(c):
        for o in order:
            x_copy(c, o).start()
        x_own(c).start()

    def forward(c, carry):
        transform(c, False)
        send(c)
        return carry

    transform(0, True)
    pl.semaphore_wait(barrier, peers + 1)
    send(0)
    if chunks > 1:
        lax.fori_loop(1, chunks, forward, 0)

    lane = lax.broadcasted_iota(jnp.int32, (half, cells), 1)

    def pack(k, carry):
        x = x_ref[k]
        top, bottom = x[:half], x[half:]
        at = pl.ds(pl.multiple_of(k * half, 8), half)
        hs[0, at, :] = jnp.where(lane < cells // 2, pltpu.roll(top, cells // 2, 1), bottom)
        hs[1, at, :] = jnp.where(lane < cells // 2, top, pltpu.roll(bottom, cells // 2, 1))
        return carry

    lax.fori_loop(0, plane_rows, pack, 0)
    side_copy(0, up).start()
    side_copy(1, down).start()

    row = lax.broadcasted_iota(jnp.int32, (points, 2 * cells), 0)
    speed = (2 * row - (points - 1)).astype(F32) * (FRICTION / points)
    cell_row = lax.broadcasted_iota(jnp.int32, (points, cells), 0)
    signed = jnp.where(cell_row < half, cell_row, cell_row - points)
    squares = signed * signed
    exact = dict(precision=lax.Precision.HIGHEST, preferred_element_type=F32)
    scale = DAMPING / (half * half)


    modes = waves_ref.shape[1]
    waves = waves_ref[...].astype(F32)
    eye = lax.broadcasted_iota(jnp.int32, (modes, modes), 0) == lax.broadcasted_iota(
        jnp.int32, (modes, modes), 1
    )

    def upright(value):
        return jnp.sum(jnp.where(eye, jnp.broadcast_to(value, (modes, modes)), 0.0), axis=1, keepdims=True)

    def turned(value, period):
        return value - period * jnp.floor(value / period)

    w_row, w_column = upright(waves[0:1]), upright(waves[1:2])
    unit = np.float32(np.pi / points)
    freq = lax.broadcasted_iota(jnp.int32, (modes, points), 1)
    freq_signed = jnp.where(freq < half, freq, freq - points).astype(F32)
    a_angle = unit * turned(w_row * freq_signed, 2.0 * points)
    a_ref[:modes] = jnp.where(freq == half, 0.0, jnp.sin(a_angle))
    a_ref[modes:] = jnp.cos(a_angle)
    rows_dev = cells // NY
    cell = lax.broadcasted_iota(jnp.int32, (modes, cells), 1).astype(F32)
    cell_line = jnp.floor(cell / NY)
    cell_column = cell - NY * cell_line
    cell_line = cell_line + (band * rows_dev).astype(F32)
    total_rows = float(rows_dev * bands)
    angles = (
        2.0 * np.pi * (turned(w_row * cell_line, total_rows) / total_rows + turned(w_column * cell_column, float(NY)) / NY)
        + upright(phase_ref[...])
    )
    cf_ref[...] = upright(amp_ref[...]) * jnp.sin(angles)

    def symbol(mode):
        b_angle = unit * turned(w_column * jnp.full((modes, cells), mode, jnp.int32).astype(F32), 2.0 * points)
        factor = jnp.concatenate([jnp.cos(b_angle) * cf_ref[...], jnp.sin(b_angle) * cf_ref[...]], axis=0)
        return lax.dot_general(a_ref[...], factor, (((0,), (0,)), ((), ())), **exact)

    def middle(c, last):
        for o in order:
            x_copy(c, o, o).wait_recv()
        x_own(c).wait()
        for i in range(PER):
            mode = me * (chunks * PER) + c * PER + i
            re = xr[c, pl.ds(2 * i, points, stride=ROWS), :]
            im = xr[c, pl.ds(2 * i + 1, points, stride=ROWS), :]
            x = jnp.concatenate([re, im], axis=1)
            pq = left_product(th_ref[...], tl_ref[...], x)
            pr, pi = pq[:points, :cells], pq[:points, cells:]
            qr, qi = pq[points:, :cells], pq[points:, cells:]
            s = symbol(mode)
            d = scale * (squares + mode * mode).astype(F32)
            xre, xim = pr + qi, pi - qr
            ur = -d * xre - s * xim
            ui = s * xre - d * xim
            vr, vi = -ui, ur
            if i == 0:
                end = symbol(-half)
                de = scale * (squares + half * half).astype(F32)
                real = mode == 0
                ur = jnp.where(real, s * qr - d * pr, ur)
                ui = jnp.where(real, end * qi - de * pi, ui)
                vr = jnp.where(real, -d * qr - s * pr, vr)
                vi = jnp.where(real, -de * qi - end * pi, vi)
            uv = jnp.concatenate(
                [jnp.concatenate([ur, ui], axis=1), jnp.concatenate([vr, vi], axis=1)], axis=0
            )
            y = left_product(ih_ref[...], il_ref[...], uv) + difference(speed * x, row, points)
            ys[c, pl.ds(2 * i, points, stride=ROWS), :] = y[:, :cells]
            ys[c, pl.ds(2 * i + 1, points, stride=ROWS), :] = y[:, cells:]
        for o in order:
            y_copy(c, o, last).start()
        y_own(c, last).start()

    def middle_step(c, carry):
        middle(c, False)
        return carry

    if chunks > 1:
        lax.fori_loop(0, chunks - 1, middle_step, 0)
    middle(chunks - 1, True)

    side_copy(0, up).wait_recv()
    side_copy(1, down).wait_recv()
    stencil = me * plane_rows // half
    cell_speed = (2 * cell_row - (points - 1)).astype(F32) / points

    def advect(g, carry):
        for a in range(block):
            k = g * block + a
            x = x_ref[k]
            at = pl.ds(pl.multiple_of(k * half, 8), half)
            top = exact_product(x[:half], plus_ref[stencil])
            bottom = exact_product(x[half:], minus_ref[stencil])
            sides = exact_product(hr[0, at, :], lt_ref[stencil]) + exact_product(hr[1, at, :], rt_ref[stencil])
            rows = jnp.concatenate(
                [top[:, :cells] + sides[:, :cells], bottom[:, :cells] + sides[:, cells:]], 0
            )
            columns = jnp.concatenate([top[:, cells:], bottom[:, cells:]], 0)
            first = (2 * (me * plane_rows + k) - (points - 1)).astype(F32) * (1.0 / points)
            acc[k] = FRICTION * difference(cell_speed * x, cell_row, points) - (
                first * rows + cell_speed * columns
            ) * (1.0 / 60.0)
        return carry

    lax.fori_loop(0, plane_rows // block, advect, 0)

    def gather(c, carry):
        for o in order:
            y_copy(c, o, False, o).wait_recv()
        y_own(c, False).wait()

        def planes(g, inner):
            for a in range(0, block, 2):
                k = g * block + a
                y = [
                    jnp.concatenate(
                        [
                            yr[c, pl.ds(pl.multiple_of((d * plane_rows + k + b) * ROWS, 8), ROWS), :]
                            for d in range(peers)
                        ],
                        axis=0,
                    )
                    for b in range(2)
                ]
                product = stacked_product(bs_ref[c], jnp.concatenate(y, axis=1))
                acc[k] += product[:, :cells]
                acc[k + 1] += product[:, cells:]
            return inner

        lax.fori_loop(0, plane_rows // block, planes, 0)
        return carry

    if chunks > 1:
        lax.fori_loop(0, chunks - 1, gather, 0)
    out = pltpu.make_async_copy(acc, out_ref, out_sem)
    out.start()

    def sent(c, carry):
        for o in order:
            x_copy(c, o).wait_send()
        return carry

    def sent_back(c, carry):
        for o in order:
            y_copy(c, o, False).wait_send()
        return carry

    lax.fori_loop(0, chunks, sent, 0)
    if chunks > 1:
        lax.fori_loop(0, chunks - 1, sent_back, 0)
    side_copy(0, up).wait_send()
    side_copy(1, down).wait_send()
    out.wait()
    for o in order:
        y_copy(chunks - 1, o, True).wait_send()
    for o in order:
        y_copy(chunks - 1, o, True, o).wait_recv()
    y_own(chunks - 1, True).wait()


def back_kernel(peers, cells, block, base_ref, table_ref, y_ref, o_ref):
    for a in range(0, block, 2):
        y = [jnp.concatenate([y_ref[d, a + b] for d in range(peers)], axis=0) for b in range(2)]
        product = stacked_product(table_ref[...], jnp.concatenate(y, axis=1))
        o_ref[a] = base_ref[a] + product[:, :cells]
        o_ref[a + 1] = base_ref[a + 1] + product[:, cells:]


def whole(shape):
    return pl.BlockSpec(shape, lambda *_: (0,) * len(shape))


def params(mib=48):
    return pltpu.CompilerParams(vmem_limit_bytes=mib * 2**20)


def cost(flops, size):
    return pl.CostEstimate(flops=int(flops), bytes_accessed=int(size), transcendentals=0)


def local(density, mode_waves, mode_amplitudes, mode_phases):
    plane_rows, points, cells = density.shape
    peers = lax.axis_size("mom")
    bands = lax.axis_size("space")
    per_peer = points // 2 // peers
    chunks = per_peer // PER
    block = 8
    steps = plane_rows // block
    half = points // 2
    size = plane_rows * points * cells * 4

    forward, back = second_tables(points, peers)
    part = peers * ROWS
    wh, wl = halves(forward)
    bh, bl = halves(np.stack([back[:, c * part : (c + 1) * part] for c in range(chunks)]))
    bs = jnp.asarray(np.concatenate([bh, bl, bh], axis=2))
    last_table = jnp.asarray(np.concatenate([bh[-1], bl[-1], bh[-1]], axis=1))
    first, inverse = first_tables(points)
    th, tl = halves(first)
    ih, il = halves(inverse)

    own_m, left_m, right_m = row_tables(cells, MINUS)
    own_p, left_p, right_p = row_tables(cells, PLUS)

    def chosen(minus, plus):
        return jnp.asarray(np.stack([plus, minus]).astype(ml_dtypes.bfloat16))

    def beside(columns):
        return chosen(np.concatenate([own_m, columns], 1), np.concatenate([own_p, columns], 1))

    vm = pl.BlockSpec(memory_space=pltpu.VMEM)
    anywhere = pl.BlockSpec(memory_space=pl.ANY)
    message_rows = peers * plane_rows * ROWS
    chunked = pltpu.VMEM((chunks, message_rows, cells), F32)
    sides = pltpu.VMEM((2, plane_rows * half, cells), F32)
    flags = pltpu.SemaphoreType.DMA((chunks, peers))
    pair = pltpu.SemaphoreType.DMA((2,))
    base, last = pl.pallas_call(
        functools.partial(exchange_kernel, peers, bands, chunks, plane_rows, points, cells),
        out_shape=[
            jax.ShapeDtypeStruct(density.shape, F32),
            jax.ShapeDtypeStruct((message_rows, cells), F32),
        ],
        in_specs=[anywhere] + [vm] * 14,
        out_specs=[anywhere] * 2,
        scratch_shapes=[chunked] * 4
        + [sides] * 2
        + [pltpu.VMEM(density.shape, F32)] * 2
        + [pltpu.VMEM((2 * mode_waves.shape[0], points), F32)]
        + [pltpu.VMEM((mode_waves.shape[0], cells), F32)]
        + [flags] * 4
        + [pair] * 2
        + [pltpu.SemaphoreType.DMA, pltpu.SemaphoreType.DMA((steps,))],
        compiler_params=pltpu.CompilerParams(
            vmem_limit_bytes=56 * 2**20, collective_id=0, has_side_effects=True
        ),
        cost_estimate=cost(3 * 3.2e9, 3 * size),
        name="exchange",
    )(
        density,
        wh,
        wl,
        th,
        tl,
        ih,
        il,
        mode_waves.T,
        mode_amplitudes.reshape(1, -1),
        mode_phases.reshape(1, -1),
        beside(column_table(cells, PLUS)),
        beside(column_table(cells, MINUS)),
        chosen(left_m, left_p),
        chosen(right_m, right_p),
        bs,
    )
    plane = lambda g: (g, 0, 0)
    return pl.pallas_call(
        functools.partial(back_kernel, peers, cells, block),
        grid=(steps,),
        out_shape=jax.ShapeDtypeStruct(density.shape, F32),
        in_specs=[
            pl.BlockSpec((block, points, cells), plane),
            whole(bs.shape[1:]),
            pl.BlockSpec((peers, block, ROWS, cells), lambda g: (0, g, 0, 0)),
        ],
        out_specs=pl.BlockSpec((block, points, cells), plane),
        compiler_params=params(60),
        cost_estimate=cost(6 * plane_rows * points * part * cells, 3 * size),
        name="second_inverse",
    )(base, last_table, last.reshape(peers, plane_rows, ROWS, cells))


def solution(mesh):
    return jax.shard_map(
        local,
        mesh=mesh,
        in_specs=(P("mom", None, "space"), P(), P(), P()),
        out_specs=P("mom", None, "space"),
        check_vma=False,
    )
```
